32 devices in a mesh: grp: 4 (over y, x), aux: 8 (over z, core).
Axes of the slice: x: 2, y: 2, z: 4, core: 2. Of those that a mesh axis runs over, the one named last changes fastest.
Arguments:
- integrals: float32 [1536, 256, 384], P('aux', 'grp'), may hold values from -0.8 to 0.8
- occ_energy: float32 [256], replicated, may hold values from -2 to -0.3
- vir_energy: float32 [384], replicated, may hold values from 0.2 to 3
- orbital_order: int32 [256], replicated, may hold values from 0 to 255, each once
- owners: int32 [1, 4], replicated, may hold values from 0 to 7, as said below
Outputs:
- density: float32 [1536, 256, 384], P('aux', 'grp')
The draws below stay inside these ranges and needn't reach their ends.
Inputs may be any that keep to these rules, and one draw needn't show every extreme that they name: `orbital_order`: a permutation of the table's entries. owners[s, g] names one of the 8 blocks of the group before g.
All inputs are finite; a program needn't handle non-finite values.
Results may differ from the reference program's by a relative error of at most 0.00011.
Values sent between devices are 32-bit elements; how exact they have to be, the bound alone decides.
No kernel may reach another device: no remote copies, remote signals or barrier semaphores. Data moves between devices by JAX's collectives and lax.ppermute only.
A program may use at most 320 MiB of HBM per device.

```python
import jax
import jax.numpy as jnp
from jax import lax

NAUX = 1536
NOCC = 256
NVIR = 384
STEPS = 1
N_GRP = 4
N_AUX = 8


def draw_owners(key, part):
    total = STEPS * N_GRP
    first_key = jax.random.fold_in(key, 11)
    second_key = jax.random.fold_in(key, 12)
    third_key = jax.random.fold_in(key, 13)
    values = jax.random.randint(first_key, (total,), 0, N_AUX, dtype=jnp.int32)
    high_spot = jax.random.randint(second_key, (), 0, total, dtype=jnp.int32)
    offset = jax.random.randint(third_key, (), 1, total, dtype=jnp.int32)
    low_spot = (high_spot + offset) % total
    places = jnp.arange(total, dtype=jnp.int32)
    values = jnp.where(places == high_spot, N_AUX - 1, values)
    values = jnp.where(places == low_spot, 0, values)
    return values.reshape(STEPS, N_GRP).astype(jnp.int32)


def shard_levels(stream_key, extent, cuts, smallest, largest):
    def one(axis_at, shards_of):
        heights = jax.random.uniform(jax.random.fold_in(jax.random.fold_in(stream_key, 6), axis_at), (shards_of,), jnp.float32, smallest / len(cuts), largest / len(cuts))
        return jnp.repeat(jnp.exp(heights), extent[axis_at] // shards_of).reshape((-1,) + (1,) * (len(extent) - axis_at - 1))

    level = one(*cuts[0])
    for cut in cuts[1:]:
        level = level * one(*cut)
    return level


def noise(own_key, dims, scale, most, cuts=(), kind=jnp.bfloat16):
    array = jax.random.normal(own_key, dims, jnp.float32) * scale
    if len(cuts) > 0:
        array = shard_levels(own_key, dims, cuts, -0.22, 0.18) * array
    return jnp.clip(array, min=-most, max=most).astype(kind)


def setup_inputs(seed: int = 0) -> dict:
    arg_keys = jax.random.split(jax.random.key(seed), 6)
    integrals = noise(arg_keys[0], (NAUX, NOCC, NVIR), 0.1, 0.8, ((0, 8), (1, 4)), jnp.float32)
    occ_energy = jnp.clip(jax.random.uniform(arg_keys[1], (NOCC,), jnp.float32, -2.0, -0.3), -2.0, -0.3)
    vir_energy = jnp.clip(jax.random.uniform(arg_keys[2], (NVIR,), jnp.float32, 0.2, 3.0), 0.2, 3.0)
    orbital_order = jax.random.permutation(arg_keys[3], NOCC).astype(jnp.int32)
    owners = draw_owners(jax.random.fold_in(arg_keys[5], 71), 0)
    return dict(integrals=integrals, occ_energy=occ_energy, vir_energy=vir_energy, orbital_order=orbital_order, owners=owners)


level_shift = 0.5


def reference(integrals, occ_energy, vir_energy, orbital_order, owners):
    highest = lax.Precision.HIGHEST
    levels = jnp.take(occ_energy, orbital_order)
    group_occ = NOCC // N_GRP
    occ_block = NOCC // (N_GRP * N_AUX)
    results = []
    for group in range(N_GRP):
        source = (group - 1) % N_GRP
        mine = integrals[:, group * group_occ:(group + 1) * group_occ, :]
        theirs = integrals[:, source * group_occ:(source + 1) * group_occ, :]
        mine_levels = levels[group * group_occ:(group + 1) * group_occ]
        their_levels = levels[source * group_occ:(source + 1) * group_occ]
        density = jnp.zeros((NAUX, group_occ, NVIR), jnp.float32)
        for step in range(STEPS):
            start = (owners[step, group] * occ_block).astype(jnp.int32)
            j_block = lax.dynamic_slice_in_dim(theirs, start, occ_block, 1)
            j_levels = lax.dynamic_slice_in_dim(their_levels, start, occ_block, 0)
            pair_ints = jnp.einsum("pia,pjb->iajb", mine, j_block, precision=highest)
            swapped = jnp.transpose(pair_ints, (0, 3, 2, 1))
            gaps = (vir_energy[None, :, None, None] + vir_energy[None, None, None, :]
                    - mine_levels[:, None, None, None] - j_levels[None, None, :, None] + level_shift)
            amplitude = (2.0 * pair_ints - swapped) / gaps
            density = density + jnp.einsum("iajb,pjb->pia", amplitude, j_block, precision=highest)
        results.append(density)
    return jnp.concatenate(results, axis=1)
```

```python
import jax
import jax.numpy as jnp
from jax import lax
from jax.experimental import pallas as pl
from jax.experimental.pallas import tpu as pltpu
from jax.sharding import PartitionSpec as P

level_shift = 0.5
vmem_bytes = 56 * 1024 * 1024


def from_behind(block, axis, distance):
    devices = range(lax.axis_size(axis))
    route = [((i - distance) % len(devices), i) for i in devices]
    return lax.ppermute(block, axis, route)


def split_bf16(x):
    high = x.astype(jnp.bfloat16)
    low = (x - high.astype(jnp.float32)).astype(jnp.bfloat16)
    return high, low


def dot3(a_high, a_low, b_high, b_low):
    def dot(a, b):
        return jnp.dot(a, b, preferred_element_type=jnp.float32)

    return dot(a_high, b_high) + (dot(a_high, b_low) + dot(a_low, b_high))


def split_j_kernel(j_ref, high_ref, low_ref):
    shards, pair, rows, n_vir = j_ref.shape
    for s in range(shards):
        for q in range(pair):
            high, low = split_bf16(j_ref[s, q])
            at = (0, pl.ds(s * rows, rows), pl.ds(q * n_vir, n_vir))
            high_ref[at] = high
            low_ref[at] = low


def split_j(gathered, pair):
    shards, n_j, rows, n_vir = gathered.shape
    shape = (n_j // pair, shards * rows, pair * n_vir)
    block = pl.BlockSpec((1,) + shape[1:], lambda k: (k, 0, 0))
    return pl.pallas_call(
        split_j_kernel,
        grid=(n_j // pair,),
        in_specs=[pl.BlockSpec((shards, pair, rows, n_vir), lambda k: (0, k, 0, 0))],
        out_specs=[block, block],
        out_shape=[jax.ShapeDtypeStruct(shape, jnp.bfloat16)] * 2,
        compiler_params=pltpu.CompilerParams(vmem_limit_bytes=vmem_bytes),
        name="split_j",
    )(gathered)


def density_kernel(i_levels, j_levels, vir_ref, high_ref, low_ref, b_ref, out_ref,
                   at_high, at_low, amp_high, amp_low):
    shards, n_i, rows, n_vir = b_ref.shape
    n_aux = shards * rows
    pair = high_ref.shape[2] // n_vir
    step = pl.program_id(0)
    merge = 1
    while (merge * rows) % 128 and merge < shards:
        merge *= 2

    @pl.when(step == 0)
    def _():
        for i in range(n_i):
            for s in range(0, shards, merge):
                part = jnp.concatenate([b_ref[s + m, i] for m in range(merge)], 0)
                high, low = split_bf16(part.T)
                at = (pl.ds(i * n_vir, n_vir), pl.ds(s * rows, merge * rows))
                at_high[at] = high
                at_low[at] = low
        out_ref[...] = jnp.zeros_like(out_ref)

    for i in range(n_i):
        mine = pl.ds(i * n_vir, n_vir)
        ints = dot3(at_high[mine, :], at_low[mine, :], high_ref[0], low_ref[0])
        for q in range(pair):
            block = ints[:, q * n_vir:(q + 1) * n_vir]
            gaps = vir_ref[...] - (i_levels[i] + j_levels[step * pair + q])
            high, low = split_bf16((2.0 * block.T - block) / gaps)
            at = (pl.ds(q * n_vir, n_vir), mine)
            amp_high[at] = high
            amp_low[at] = low

    @pl.loop(0, shards // merge)
    def _(s):
        at = pl.ds(pl.multiple_of(s * (merge * rows), merge * rows), merge * rows)
        part = dot3(high_ref[0, at, :], low_ref[0, at, :], amp_high[...], amp_low[...])
        for m in range(merge):
            for i in range(n_i):
                out_ref[s * merge + m, i] += part[m * rows:(m + 1) * rows, i * n_vir:(i + 1) * n_vir]


def block_density(i_levels, j_levels, vir_pair, j_high, j_low, b_block):
    shards, n_i, rows, n_vir = b_block.shape
    steps, n_aux, width = j_high.shape
    whole = lambda shape: pl.BlockSpec(shape, lambda k: (0,) * len(shape))
    smem = pl.BlockSpec(memory_space=pltpu.SMEM)
    j_spec = pl.BlockSpec((1, n_aux, width), lambda k: (k, 0, 0))
    flops = 2 * 2 * 3 * n_aux * n_i * n_vir * steps * width
    return pl.pallas_call(
        density_kernel,
        grid=(steps,),
        in_specs=[smem, smem, whole(vir_pair.shape), j_spec, j_spec, whole(b_block.shape)],
        out_specs=whole(b_block.shape),
        out_shape=jax.ShapeDtypeStruct(b_block.shape, jnp.float32),
        scratch_shapes=[
            pltpu.VMEM((n_i * n_vir, n_aux), jnp.bfloat16),
            pltpu.VMEM((n_i * n_vir, n_aux), jnp.bfloat16),
            pltpu.VMEM((width, n_i * n_vir), jnp.bfloat16),
            pltpu.VMEM((width, n_i * n_vir), jnp.bfloat16),
        ],
        compiler_params=pltpu.CompilerParams(vmem_limit_bytes=vmem_bytes),
        cost_estimate=pl.CostEstimate(
            flops=flops, bytes_accessed=4 * steps * n_aux * width + 8 * b_block.size,
            transcendentals=0),
        name="block_density",
    )(i_levels, j_levels, vir_pair, j_high, j_low, b_block)


def place_kernel(part_ref, *refs):
    out_ref = refs[-1]
    for i in range(part_ref.shape[0]):
        out_ref[:, i, :] = part_ref[i]


def place(part, out, shape, start):
    n_i, rows, n_vir = part.shape
    step = 8 if n_i % 8 == 0 else n_i
    out_block = pl.BlockSpec((rows, step, n_vir), lambda k: (0, start // step + k, 0))
    operands = [part]
    in_specs = [pl.BlockSpec((step, rows, n_vir), lambda k: (k, 0, 0))]
    aliases = {}
    if out is not None:
        operands.append(out)
        in_specs.append(pl.BlockSpec(memory_space=pl.ANY))
        aliases = {1: 0}
    return pl.pallas_call(
        place_kernel,
        grid=(n_i // step,),
        in_specs=in_specs,
        out_specs=out_block,
        out_shape=jax.ShapeDtypeStruct(shape, jnp.float32),
        input_output_aliases=aliases,
        compiler_params=pltpu.CompilerParams(vmem_limit_bytes=vmem_bytes),
        name="place",
    )(*operands)


def body(integrals, occ_energy, vir_energy, orbital_order, owners):
    n_groups = lax.axis_size("grp")
    n_shards = lax.axis_size("aux")
    grp_index = lax.axis_index("grp")
    aux_index = lax.axis_index("aux")
    rows, group_occ, n_vir = integrals.shape
    n_occ = occ_energy.shape[0]
    occ_block = group_occ // n_shards
    n_i = 2 if occ_block % 2 == 0 else 1
    chunk = n_shards * n_i

    onehot = orbital_order[:, None] == jnp.arange(n_occ, dtype=jnp.int32)[None, :]
    levels = jnp.sum(jnp.where(onehot, occ_energy[None, :], 0.0), axis=1)
    vir_pair = vir_energy[:, None] + vir_energy[None, :] + level_shift

    source_group = (grp_index + n_groups - 1) % n_groups
    next_group = (grp_index + 1) % n_groups
    my_owner = lax.dynamic_index_in_dim(owners[0], grp_index, 0, keepdims=False)
    next_owner = lax.dynamic_index_in_dim(owners[0], next_group, 0, keepdims=False)
    sent = lax.dynamic_slice_in_dim(integrals, next_owner * occ_block, occ_block, 1)
    arrived = from_behind(jnp.transpose(sent, (1, 0, 2)), "grp", 1)
    gathered = lax.all_gather(arrived, "aux", axis=0, tiled=False)
    j_levels = lax.dynamic_slice_in_dim(
        levels, source_group * group_occ + my_owner * occ_block, occ_block, 0)
    pair = 2 if occ_block % 2 == 0 else 1

    starts = range(0, group_occ, chunk)
    blocks = []
    for start in starts:
        part = jnp.transpose(integrals[:, start:start + chunk, :], (1, 0, 2))
        part = part.reshape(n_shards, n_i, rows, n_vir)
        blocks.append(lax.all_to_all(part, "aux", split_axis=0, concat_axis=0, tiled=True))
    j_high, j_low = split_j(gathered, pair)
    out = None
    for start, block in zip(starts, blocks):
        i_levels = lax.dynamic_slice_in_dim(
            levels, grp_index * group_occ + start + aux_index * n_i, n_i, 0)
        density = block_density(i_levels, j_levels, vir_pair, j_high, j_low, block)
        back = lax.all_to_all(density, "aux", split_axis=0, concat_axis=0, tiled=True)
        out = place(back.reshape(chunk, rows, n_vir), out, integrals.shape, start)
    return out


def solution(mesh):
    in_specs = (P("aux", "grp", None), P(), P(), P(), P())
    out_specs = P("aux", "grp", None)
    return jax.shard_map(body, mesh=mesh, in_specs=in_specs, out_specs=out_specs, check_vma=False)
```

```python
import jax
import jax.numpy as jnp
from jax import lax
from jax.experimental import pallas as pl
from jax.experimental.pallas import tpu as pltpu
from jax.sharding import PartitionSpec as P

level_shift = 0.5
vmem_bytes = 56 * 1024 * 1024


def from_behind(block, axis, distance):
    devices = range(lax.axis_size(axis))
    route = [((i - distance) % len(devices), i) for i in devices]
    return lax.ppermute(block, axis, route)


def split_bf16(x):
    high = x.astype(jnp.bfloat16)
    low = (x - high.astype(jnp.float32)).astype(jnp.bfloat16)
    return high, low


def dot3(a_high, a_low, b_high, b_low):
    def dot(a, b):
        return jnp.dot(a, b, preferred_element_type=jnp.float32)

    return dot(a_high, b_high) + (dot(a_high, b_low) + dot(a_low, b_high))


def split_j_kernel(j_ref, high_ref, low_ref):
    shards, pair, rows, n_vir = j_ref.shape
    for s in range(shards):
        for q in range(pair):
            high, low = split_bf16(j_ref[s, q])
            at = (0, pl.ds(s * rows, rows), pl.ds(q * n_vir, n_vir))
            high_ref[at] = high
            low_ref[at] = low


def split_j(gathered, pair):
    shards, n_j, rows, n_vir = gathered.shape
    shape = (n_j // pair, shards * rows, pair * n_vir)
    block = pl.BlockSpec((1,) + shape[1:], lambda k: (k, 0, 0))
    return pl.pallas_call(
        split_j_kernel,
        grid=(n_j // pair,),
        in_specs=[pl.BlockSpec((shards, pair, rows, n_vir), lambda k: (0, k, 0, 0))],
        out_specs=[block, block],
        out_shape=[jax.ShapeDtypeStruct(shape, jnp.bfloat16)] * 2,
        compiler_params=pltpu.CompilerParams(vmem_limit_bytes=vmem_bytes),
        name="split_j",
    )(gathered)


def density_kernel(i_levels, j_levels, vir_ref, high_ref, low_ref, b_ref, out_ref,
                   at_high, at_low, amp_high, amp_low):
    shards, n_i, rows, n_vir = b_ref.shape
    n_aux = shards * rows
    pair = high_ref.shape[2] // n_vir
    step = pl.program_id(0)
    merge = 1
    while (merge * rows) % 128 and merge < shards:
        merge *= 2

    @pl.when(step == 0)
    def _():
        for i in range(n_i):
            for s in range(0, shards, merge):
                part = jnp.concatenate([b_ref[s + m, i] for m in range(merge)], 0)
                high, low = split_bf16(part.T)
                at = (pl.ds(i * n_vir, n_vir), pl.ds(s * rows, merge * rows))
                at_high[at] = high
                at_low[at] = low
        out_ref[...] = jnp.zeros_like(out_ref)

    for i in range(n_i):
        mine = pl.ds(i * n_vir, n_vir)
        ints = dot3(at_high[mine, :], at_low[mine, :], high_ref[0], low_ref[0])
        for q in range(pair):
            block = ints[:, q * n_vir:(q + 1) * n_vir]
            gaps = vir_ref[...] - (i_levels[i] + j_levels[step * pair + q])
            high, low = split_bf16((2.0 * block.T - block) / gaps)
            at = (pl.ds(q * n_vir, n_vir), mine)
            amp_high[at] = high
            amp_low[at] = low

    @pl.loop(0, shards // merge)
    def _(s):
        at = pl.ds(pl.multiple_of(s * (merge * rows), merge * rows), merge * rows)
        part = dot3(high_ref[0, at, :], low_ref[0, at, :], amp_high[...], amp_low[...])
        for m in range(merge):
            for i in range(n_i):
                out_ref[s * merge + m, i] += part[m * rows:(m + 1) * rows, i * n_vir:(i + 1) * n_vir]


def block_density(i_levels, j_levels, vir_pair, j_high, j_low, b_block):
    shards, n_i, rows, n_vir = b_block.shape
    steps, n_aux, width = j_high.shape
    whole = lambda shape: pl.BlockSpec(shape, lambda k: (0,) * len(shape))
    smem = pl.BlockSpec(memory_space=pltpu.SMEM)
    j_spec = pl.BlockSpec((1, n_aux, width), lambda k: (k, 0, 0))
    flops = 2 * 2 * 3 * n_aux * n_i * n_vir * steps * width
    return pl.pallas_call(
        density_kernel,
        grid=(steps,),
        in_specs=[smem, smem, whole(vir_pair.shape), j_spec, j_spec, whole(b_block.shape)],
        out_specs=whole(b_block.shape),
        out_shape=jax.ShapeDtypeStruct(b_block.shape, jnp.float32),
        scratch_shapes=[
            pltpu.VMEM((n_i * n_vir, n_aux), jnp.bfloat16),
            pltpu.VMEM((n_i * n_vir, n_aux), jnp.bfloat16),
            pltpu.VMEM((width, n_i * n_vir), jnp.bfloat16),
            pltpu.VMEM((width, n_i * n_vir), jnp.bfloat16),
        ],
        compiler_params=pltpu.CompilerParams(vmem_limit_bytes=vmem_bytes),
        cost_estimate=pl.CostEstimate(
            flops=flops, bytes_accessed=4 * steps * n_aux * width + 8 * b_block.size,
            transcendentals=0),
        name="block_density",
    )(i_levels, j_levels, vir_pair, j_high, j_low, b_block)


def pack_kernel(at_ref, in_ref, out_ref):
    for t in range(in_ref.shape[1]):
        out_ref[t, 0] = in_ref[:, t, :]


def pack(integrals, places, width):
    rows, _, n_vir = integrals.shape
    n_i = places.shape[0]
    cuts = 2 if rows % 16 == 0 else 1
    tile = rows // cuts
    return pl.pallas_call(
        pack_kernel,
        grid_spec=pltpu.PrefetchScalarGridSpec(
            num_scalar_prefetch=1,
            grid=(n_i, cuts),
            in_specs=[pl.BlockSpec((tile, width, n_vir), lambda m, r, at: (r, at[m], 0))],
            out_specs=pl.BlockSpec((width, 1, tile, n_vir), lambda m, r, at: (0, m, r, 0)),
        ),
        out_shape=jax.ShapeDtypeStruct((width, n_i, rows, n_vir), jnp.float32),
        compiler_params=pltpu.CompilerParams(vmem_limit_bytes=vmem_bytes),
        cost_estimate=pl.CostEstimate(
            flops=0, bytes_accessed=8 * width * n_i * rows * n_vir, transcendentals=0),
        name="pack",
    )(places, integrals)


def place_kernel(at_ref, part_ref, *refs):
    out_ref = refs[-1]
    for t in range(part_ref.shape[0]):
        out_ref[:, t, :] = part_ref[t, 0]


def place(part, places, out, shape):
    width, n_i, rows, n_vir = part.shape
    cuts = 2 if rows % 16 == 0 else 1
    tile = rows // cuts
    operands = [places, part]
    in_specs = [pl.BlockSpec((width, 1, tile, n_vir), lambda m, r, at: (0, m, r, 0))]
    aliases = {}
    if out is not None:
        operands.append(out)
        in_specs.append(pl.BlockSpec(memory_space=pl.ANY))
        aliases = {2: 0}
    return pl.pallas_call(
        place_kernel,
        grid_spec=pltpu.PrefetchScalarGridSpec(
            num_scalar_prefetch=1,
            grid=(n_i, cuts),
            in_specs=in_specs,
            out_specs=pl.BlockSpec((tile, width, n_vir), lambda m, r, at: (r, at[m], 0)),
        ),
        out_shape=jax.ShapeDtypeStruct(shape, jnp.float32),
        input_output_aliases=aliases,
        compiler_params=pltpu.CompilerParams(vmem_limit_bytes=vmem_bytes),
        cost_estimate=pl.CostEstimate(
            flops=0, bytes_accessed=8 * width * n_i * rows * n_vir, transcendentals=0),
        name="place",
    )(*operands)


def join_j_kernel(at_ref, *refs):
    high_ref, low_ref = refs[-2:]
    n_half = (len(refs) - 2) // 3
    near, cross, late = refs[:n_half], refs[n_half:2 * n_half], refs[2 * n_half:3 * n_half]
    rows, n_vir = near[0].shape[1:]
    step = pl.program_id(0)
    me = at_ref[0]
    far_start = (1 - me // n_half) * n_half

    def put(x, shard, q):
        high, low = split_bf16(x)
        at = (0, pl.ds(pl.multiple_of(shard * rows, rows), rows), pl.ds(q * n_vir, n_vir))
        high_ref[at] = high
        low_ref[at] = low

    for q in range(2):
        @pl.when(step % 2 == q)
        def _(q=q):
            for d in range(n_half):
                put(near[d][0], me ^ d, q)

            @pl.when(step < n_half)
            def _():
                for d in range(n_half):
                    put(cross[d][0], me ^ d ^ n_half, q)

            for d in range(n_half):
                if d % 2 == q:
                    @pl.when(step == n_half + d)
                    def _(d=d):
                        for s in range(n_half):
                            put(late[d][s], far_start + s, q)


def join_j(me, order, near, cross, late):
    n_half = len(near)
    n_j, rows, n_vir = near[0].shape
    shape = (n_j // 2, 2 * n_half * rows, 2 * n_vir)
    out_block = pl.BlockSpec((1,) + shape[1:], lambda k, at: (k // 2, 0, 0))
    in_specs = (
        [pl.BlockSpec((1, rows, n_vir), lambda k, at: (at[1 + k], 0, 0))] * n_half
        + [pl.BlockSpec((1, rows, n_vir), lambda k, at: (jnp.minimum(k, n_half - 1), 0, 0))] * n_half
        + [pl.BlockSpec((n_half, rows, n_vir), lambda k, at: (0, 0, 0))] * n_half
    )
    return pl.pallas_call(
        join_j_kernel,
        grid_spec=pltpu.PrefetchScalarGridSpec(
            num_scalar_prefetch=1,
            grid=(n_j,),
            in_specs=in_specs,
            out_specs=[out_block, out_block],
        ),
        out_shape=[jax.ShapeDtypeStruct(shape, jnp.bfloat16)] * 2,
        compiler_params=pltpu.CompilerParams(vmem_limit_bytes=vmem_bytes),
        cost_estimate=pl.CostEstimate(
            flops=0, bytes_accessed=8 * n_j * 2 * n_half * rows * n_vir, transcendentals=0),
        name="join_j",
    )(jnp.concatenate([me[None], order]), *near, *cross, *late)


def across(block, distance):
    route = [(i, i ^ distance) for i in range(lax.axis_size("aux"))]
    return lax.ppermute(block, "aux", route)


def within_half(block, n_half):
    found = [block]
    for d in range(1, n_half):
        low = d & -d
        found.append(across(found[d ^ low], low))
    return found


def pick(table, index):
    chosen = index[:, None] == jnp.arange(table.shape[0], dtype=jnp.int32)[None, :]
    return jnp.sum(jnp.where(chosen, table[None, :], 0.0), axis=1)


def body(integrals, occ_energy, vir_energy, orbital_order, owners):
    n_groups = lax.axis_size("grp")
    n_shards = lax.axis_size("aux")
    grp_index = lax.axis_index("grp").astype(jnp.int32)
    me = lax.axis_index("aux").astype(jnp.int32)
    rows, group_occ, n_vir = integrals.shape
    occ_block = group_occ // n_shards
    n_half = n_shards // 2
    shared = occ_block == n_shards and n_half >= 2 and n_shards & (n_shards - 1) == 0

    source_group = (grp_index + n_groups - 1) % n_groups
    next_group = (grp_index + 1) % n_groups
    my_owner = lax.dynamic_index_in_dim(owners[0], grp_index, 0, keepdims=False)
    next_owner = lax.dynamic_index_in_dim(owners[0], next_group, 0, keepdims=False)

    n_blocks = group_occ // n_shards
    first = next_owner if shared else jnp.int32(0)
    places = (first + jnp.arange(n_blocks, dtype=jnp.int32)) % n_blocks
    n_i = 2 if n_blocks % 2 == 0 else 1
    chunks = [places[m:m + n_i] for m in range(0, n_blocks, n_i)]

    def send_in(part):
        return lax.all_to_all(part, "aux", split_axis=0, concat_axis=0, tiled=True)

    parts = [pack(integrals, chunk, n_shards) for chunk in chunks]
    blocks = [send_in(parts[0])]

    def send_after(c, *done):
        if c < len(parts):
            part = lax.optimization_barrier((parts[c],) + done)[0]
            blocks.append(send_in(part))

    sent = lax.dynamic_slice_in_dim(integrals, next_owner * occ_block, occ_block, 1)
    arrived = from_behind(jnp.transpose(sent, (1, 0, 2)), "grp", 1)
    natural = jnp.arange(occ_block, dtype=jnp.int32)
    if shared:
        half = me // n_half
        far_start = (1 - half) * n_half
        near = within_half(arrived, n_half)
        crossing = lax.dynamic_slice_in_dim(arrived, half * n_half, n_half, 0)
        crossed = across(crossing, n_half)
        cross = within_half(crossed, n_half)
        send_after(1, arrived)
        owned = lax.dynamic_slice(
            blocks[0], (far_start, 0, 0, 0), (n_half, 1, rows, n_vir)).reshape(n_half, rows, n_vir)
        late_own = from_behind(owned, "grp", 1)
        late = within_half(late_own, n_half)
        send_after(2, near[n_half // 2], crossed, late_own)
        send_after(3, *near, *cross, *late)
        order = jnp.where(natural < n_half, far_start + natural, me ^ (natural - n_half))
        j_high, j_low = join_j(me, order, near, cross, late)
    else:
        order = natural
        gathered = lax.all_gather(arrived, "aux", axis=0, tiled=False)
        j_high, j_low = split_j(gathered, 2 if occ_block % 2 == 0 else 1)
    for c in range(len(blocks), len(parts)):
        send_after(c)

    levels = pick(occ_energy, orbital_order)
    vir_pair = vir_energy[:, None] + vir_energy[None, :] + level_shift
    j_levels = pick(levels, source_group * group_occ + my_owner * occ_block + order)
    i_levels = pick(levels, grp_index * group_occ + places * n_shards + me)

    out = None
    for c, (chunk, block) in enumerate(zip(chunks, blocks)):
        density = block_density(
            i_levels[c * n_i:(c + 1) * n_i], j_levels, vir_pair, j_high, j_low, block)
        back = lax.all_to_all(density, "aux", split_axis=0, concat_axis=0, tiled=True)
        out = place(back, chunk, out, integrals.shape)
    return out


def solution(mesh):
    in_specs = (P("aux", "grp", None), P(), P(), P(), P())
    out_specs = P("aux", "grp", None)
    return jax.shard_map(body, mesh=mesh, in_specs=in_specs, out_specs=out_specs, check_vma=False)
```

```python
import jax
import jax.numpy as jnp
from jax import lax
from jax.experimental import pallas as pl
from jax.experimental.pallas import tpu as pltpu
from jax.sharding import PartitionSpec as P

level_shift = 0.5
vmem_bytes = 56 * 1024 * 1024


def from_behind(block, axis, distance):
    devices = range(lax.axis_size(axis))
    route = [((i - distance) % len(devices), i) for i in devices]
    return lax.ppermute(block, axis, route)


def split_bf16(x):
    high = x.astype(jnp.bfloat16)
    low = (x - high.astype(jnp.float32)).astype(jnp.bfloat16)
    return high, low


def dot3(a_high, a_low, b_high, b_low):
    def dot(a, b):
        return jnp.dot(a, b, preferred_element_type=jnp.float32)

    return dot(a_high, b_high) + (dot(a_high, b_low) + dot(a_low, b_high))


def split_j_kernel(j_ref, high_ref, low_ref):
    shards, pair, rows, n_vir = j_ref.shape
    for s in range(shards):
        for q in range(pair):
            high, low = split_bf16(j_ref[s, q])
            at = (0, pl.ds(s * rows, rows), pl.ds(q * n_vir, n_vir))
            high_ref[at] = high
            low_ref[at] = low


def split_j(gathered, pair):
    shards, n_j, rows, n_vir = gathered.shape
    shape = (n_j // pair, shards * rows, pair * n_vir)
    block = pl.BlockSpec((1,) + shape[1:], lambda k: (k, 0, 0))
    return pl.pallas_call(
        split_j_kernel,
        grid=(n_j // pair,),
        in_specs=[pl.BlockSpec((shards, pair, rows, n_vir), lambda k: (0, k, 0, 0))],
        out_specs=[block, block],
        out_shape=[jax.ShapeDtypeStruct(shape, jnp.bfloat16)] * 2,
        compiler_params=pltpu.CompilerParams(vmem_limit_bytes=vmem_bytes),
        name="split_j",
    )(gathered)


def density_kernel(i_levels, j_levels, vir_ref, high_ref, low_ref, b_ref, out_ref,
                   at_high, at_low, amp_high, amp_low):
    shards, n_i, rows, n_vir = b_ref.shape
    n_aux = shards * rows
    pair = high_ref.shape[2] // n_vir
    step = pl.program_id(1)
    merge = 1
    while (merge * rows) % 128 and merge < shards:
        merge *= 2

    @pl.when(step == 0)
    def _():
        for i in range(n_i):
            for s in range(0, shards, merge):
                part = jnp.concatenate([b_ref[s + m, i] for m in range(merge)], 0)
                high, low = split_bf16(part.T)
                at = (pl.ds(i * n_vir, n_vir), pl.ds(s * rows, merge * rows))
                at_high[at] = high
                at_low[at] = low
        out_ref[...] = jnp.zeros_like(out_ref)

    for i in range(n_i):
        mine = pl.ds(i * n_vir, n_vir)
        ints = dot3(at_high[mine, :], at_low[mine, :], high_ref[0], low_ref[0])
        for q in range(pair):
            block = ints[:, q * n_vir:(q + 1) * n_vir]
            gaps = vir_ref[...] - (i_levels[pl.program_id(0) * n_i + i] + j_levels[step * pair + q])
            high, low = split_bf16((2.0 * block.T - block) / gaps)
            at = (pl.ds(q * n_vir, n_vir), mine)
            amp_high[at] = high
            amp_low[at] = low

    @pl.loop(0, shards // merge)
    def _(s):
        at = pl.ds(pl.multiple_of(s * (merge * rows), merge * rows), merge * rows)
        part = dot3(high_ref[0, at, :], low_ref[0, at, :], amp_high[...], amp_low[...])
        for m in range(merge):
            for i in range(n_i):
                out_ref[s * merge + m, i] += part[m * rows:(m + 1) * rows, i * n_vir:(i + 1) * n_vir]


def block_density(i_levels, j_levels, vir_pair, j_high, j_low, b_block):
    shards, n_i, rows, n_vir = b_block.shape
    steps, n_aux, width = j_high.shape
    at_once = 2 if n_i % 2 == 0 else 1
    smem = pl.BlockSpec(memory_space=pltpu.SMEM)
    vir_spec = pl.BlockSpec(vir_pair.shape, lambda h, k: (0, 0))
    j_spec = pl.BlockSpec((1, n_aux, width), lambda h, k: (k, 0, 0))
    b_spec = pl.BlockSpec((shards, at_once, rows, n_vir), lambda h, k: (0, h, 0, 0))
    flops = 2 * 2 * 3 * n_aux * n_i * n_vir * steps * width
    return pl.pallas_call(
        density_kernel,
        grid=(n_i // at_once, steps),
        in_specs=[smem, smem, vir_spec, j_spec, j_spec, b_spec],
        out_specs=b_spec,
        out_shape=jax.ShapeDtypeStruct(b_block.shape, jnp.float32),
        scratch_shapes=[
            pltpu.VMEM((at_once * n_vir, n_aux), jnp.bfloat16),
            pltpu.VMEM((at_once * n_vir, n_aux), jnp.bfloat16),
            pltpu.VMEM((width, at_once * n_vir), jnp.bfloat16),
            pltpu.VMEM((width, at_once * n_vir), jnp.bfloat16),
        ],
        compiler_params=pltpu.CompilerParams(vmem_limit_bytes=vmem_bytes),
        cost_estimate=pl.CostEstimate(
            flops=flops, bytes_accessed=4 * steps * n_aux * width + 8 * b_block.size,
            transcendentals=0),
        name="block_density",
    )(i_levels, j_levels, vir_pair, j_high, j_low, b_block)


def pack_kernel(at_ref, in_ref, out_ref):
    for t in range(in_ref.shape[1]):
        out_ref[t, 0] = in_ref[:, t, :]


def pack(integrals, places, width):
    rows, _, n_vir = integrals.shape
    n_i = places.shape[0]
    cuts = 2 if rows % 16 == 0 else 1
    tile = rows // cuts
    return pl.pallas_call(
        pack_kernel,
        grid_spec=pltpu.PrefetchScalarGridSpec(
            num_scalar_prefetch=1,
            grid=(n_i, cuts),
            in_specs=[pl.BlockSpec((tile, width, n_vir), lambda m, r, at: (r, at[m], 0))],
            out_specs=pl.BlockSpec((width, 1, tile, n_vir), lambda m, r, at: (0, m, r, 0)),
        ),
        out_shape=jax.ShapeDtypeStruct((width, n_i, rows, n_vir), jnp.float32),
        compiler_params=pltpu.CompilerParams(vmem_limit_bytes=vmem_bytes),
        cost_estimate=pl.CostEstimate(
            flops=0, bytes_accessed=8 * width * n_i * rows * n_vir, transcendentals=0),
        name="pack",
    )(places, integrals)


def place_kernel(at_ref, part_ref, *refs):
    out_ref = refs[-1]
    for t in range(part_ref.shape[0]):
        out_ref[:, t, :] = part_ref[t, 0]


def place(part, places, out, shape):
    width, n_i, rows, n_vir = part.shape
    cuts = 2 if rows % 16 == 0 else 1
    tile = rows // cuts
    operands = [places, part]
    in_specs = [pl.BlockSpec((width, 1, tile, n_vir), lambda m, r, at: (0, m, r, 0))]
    aliases = {}
    if out is not None:
        operands.append(out)
        in_specs.append(pl.BlockSpec(memory_space=pl.ANY))
        aliases = {2: 0}
    return pl.pallas_call(
        place_kernel,
        grid_spec=pltpu.PrefetchScalarGridSpec(
            num_scalar_prefetch=1,
            grid=(n_i, cuts),
            in_specs=in_specs,
            out_specs=pl.BlockSpec((tile, width, n_vir), lambda m, r, at: (r, at[m], 0)),
        ),
        out_shape=jax.ShapeDtypeStruct(shape, jnp.float32),
        input_output_aliases=aliases,
        compiler_params=pltpu.CompilerParams(vmem_limit_bytes=vmem_bytes),
        cost_estimate=pl.CostEstimate(
            flops=0, bytes_accessed=8 * width * n_i * rows * n_vir, transcendentals=0),
        name="place",
    )(*operands)


def join_j_kernel(at_ref, *refs):
    high_ref, low_ref = refs[-2:]
    n_half = (len(refs) - 2) // 3
    near, cross, late = refs[:n_half], refs[n_half:2 * n_half], refs[2 * n_half:3 * n_half]
    rows, n_vir = near[0].shape[1:]
    step = pl.program_id(0)
    me = at_ref[0]
    far_start = (1 - me // n_half) * n_half

    def put(x, shard, q):
        high, low = split_bf16(x)
        at = (0, pl.ds(pl.multiple_of(shard * rows, rows), rows), pl.ds(q * n_vir, n_vir))
        high_ref[at] = high
        low_ref[at] = low

    for q in range(2):
        @pl.when(step % 2 == q)
        def _(q=q):
            for d in range(n_half):
                put(near[d][0], me ^ d, q)

            @pl.when(step < n_half)
            def _():
                for d in range(n_half):
                    put(cross[d][0], me ^ d ^ n_half, q)

            for d in range(n_half):
                if d % 2 == q:
                    @pl.when(step == n_half + d)
                    def _(d=d):
                        for s in range(n_half):
                            put(late[d][s], far_start + s, q)


def join_j(me, order, near, cross, late):
    n_half = len(near)
    n_j, rows, n_vir = near[0].shape
    shape = (n_j // 2, 2 * n_half * rows, 2 * n_vir)
    out_block = pl.BlockSpec((1,) + shape[1:], lambda k, at: (k // 2, 0, 0))
    in_specs = (
        [pl.BlockSpec((1, rows, n_vir), lambda k, at: (at[1 + k], 0, 0))] * n_half
        + [pl.BlockSpec((1, rows, n_vir), lambda k, at: (jnp.minimum(k, n_half - 1), 0, 0))] * n_half
        + [pl.BlockSpec((n_half, rows, n_vir), lambda k, at: (0, 0, 0))] * n_half
    )
    return pl.pallas_call(
        join_j_kernel,
        grid_spec=pltpu.PrefetchScalarGridSpec(
            num_scalar_prefetch=1,
            grid=(n_j,),
            in_specs=in_specs,
            out_specs=[out_block, out_block],
        ),
        out_shape=[jax.ShapeDtypeStruct(shape, jnp.bfloat16)] * 2,
        compiler_params=pltpu.CompilerParams(vmem_limit_bytes=vmem_bytes),
        cost_estimate=pl.CostEstimate(
            flops=0, bytes_accessed=8 * n_j * 2 * n_half * rows * n_vir, transcendentals=0),
        name="join_j",
    )(jnp.concatenate([me[None], order]), *near, *cross, *late)


def across(block, distance):
    route = [(i, i ^ distance) for i in range(lax.axis_size("aux"))]
    return lax.ppermute(block, "aux", route)


def within_half(block, n_half):
    found = [block]
    for d in range(1, n_half):
        low = d & -d
        found.append(across(found[d ^ low], low))
    return found


def pick(table, index):
    chosen = index[:, None] == jnp.arange(table.shape[0], dtype=jnp.int32)[None, :]
    return jnp.sum(jnp.where(chosen, table[None, :], 0.0), axis=1)


def body(integrals, occ_energy, vir_energy, orbital_order, owners):
    n_groups = lax.axis_size("grp")
    n_shards = lax.axis_size("aux")
    grp_index = lax.axis_index("grp").astype(jnp.int32)
    me = lax.axis_index("aux").astype(jnp.int32)
    rows, group_occ, n_vir = integrals.shape
    occ_block = group_occ // n_shards
    n_half = n_shards // 2
    shared = occ_block == n_shards and n_half >= 2 and n_shards & (n_shards - 1) == 0

    source_group = (grp_index + n_groups - 1) % n_groups
    next_group = (grp_index + 1) % n_groups
    my_owner = lax.dynamic_index_in_dim(owners[0], grp_index, 0, keepdims=False)
    next_owner = lax.dynamic_index_in_dim(owners[0], next_group, 0, keepdims=False)

    n_blocks = group_occ // n_shards
    first = next_owner if shared else jnp.int32(0)
    places = (first + jnp.arange(n_blocks, dtype=jnp.int32)) % n_blocks
    n_i = 2 if n_blocks % 2 == 0 else 1
    ends = [0, n_i, n_blocks - n_i, n_blocks] if n_blocks >= 3 * n_i else [0, n_blocks]
    chunks = [places[start:end] for start, end in zip(ends, ends[1:])]

    def send_in(part):
        return lax.all_to_all(part, "aux", split_axis=0, concat_axis=0, tiled=True)

    parts = [pack(integrals, chunk, n_shards) for chunk in chunks]
    blocks = [send_in(parts[0])]
    sent = lax.dynamic_slice_in_dim(integrals, next_owner * occ_block, occ_block, 1)
    arrived = from_behind(jnp.transpose(sent, (1, 0, 2)), "grp", 1)
    if len(parts) > 1:
        bound = lax.optimization_barrier((arrived, *parts[1:]))
        arrived, parts[1:] = bound[0], bound[1:]

    def send_after(c, *done):
        if c < len(parts):
            part = lax.optimization_barrier((parts[c], blocks[c - 1]) + done)[0]
            blocks.append(send_in(part))

    natural = jnp.arange(occ_block, dtype=jnp.int32)
    if shared:
        half = me // n_half
        far_start = (1 - half) * n_half
        near = within_half(arrived, n_half)
        crossing = lax.dynamic_slice_in_dim(arrived, half * n_half, n_half, 0)
        crossed = across(crossing, n_half)
        send_after(1, near[n_half // 2], crossed)
        owned = lax.dynamic_slice(
            blocks[0], (far_start, 0, 0, 0), (n_half, 1, rows, n_vir)).reshape(n_half, rows, n_vir)
        late_own = from_behind(owned, "grp", 1)
        crossed = lax.optimization_barrier((crossed, late_own))[0]
        cross = within_half(crossed, n_half)
        late = within_half(late_own, n_half)
        send_after(2, *near, *cross, *late)
        order = jnp.where(natural < n_half, far_start + natural, me ^ (natural - n_half))
        j_high, j_low = join_j(me, order, near, cross, late)
    else:
        order = natural
        gathered = lax.all_gather(arrived, "aux", axis=0, tiled=False)
        j_high, j_low = split_j(gathered, 2 if occ_block % 2 == 0 else 1)
    for c in range(len(blocks), len(parts)):
        send_after(c)

    levels = pick(occ_energy, orbital_order)
    vir_pair = vir_energy[:, None] + vir_energy[None, :] + level_shift
    j_levels = pick(levels, source_group * group_occ + my_owner * occ_block + order)
    i_levels = pick(levels, grp_index * group_occ + places * n_shards + me)

    out = None
    for c, (chunk, block) in enumerate(zip(chunks, blocks)):
        density = block_density(
            i_levels[ends[c]:ends[c + 1]], j_levels, vir_pair, j_high, j_low, block)
        density = lax.optimization_barrier((density, blocks[-1]))[0]
        back = lax.all_to_all(density, "aux", split_axis=0, concat_axis=0, tiled=True)
        out = place(back, chunk, out, integrals.shape)
    return out


def solution(mesh):
    in_specs = (P("aux", "grp", None), P(), P(), P(), P())
    out_specs = P("aux", "grp", None)
    return jax.shard_map(body, mesh=mesh, in_specs=in_specs, out_specs=out_specs, check_vma=False)
```

```python
import jax
import jax.numpy as jnp
from jax import lax
from jax.experimental import pallas as pl
from jax.experimental.pallas import tpu as pltpu
from jax.sharding import PartitionSpec as P

level_shift = 0.5
vmem_bytes = 56 * 1024 * 1024


def from_behind(block, axis, distance):
    devices = range(lax.axis_size(axis))
    route = [((i - distance) % len(devices), i) for i in devices]
    return lax.ppermute(block, axis, route)


def split_bf16(x):
    high = x.astype(jnp.bfloat16)
    low = (x - high.astype(jnp.float32)).astype(jnp.bfloat16)
    return high, low


def dot3(a_high, a_low, b_high, b_low):
    def dot(a, b):
        return jnp.dot(a, b, preferred_element_type=jnp.float32)

    return dot(a_high, b_high) + (dot(a_high, b_low) + dot(a_low, b_high))


def split_j_kernel(j_ref, high_ref, low_ref):
    shards, pair, rows, n_vir = j_ref.shape
    for s in range(shards):
        for q in range(pair):
            high, low = split_bf16(j_ref[s, q])
            at = (0, pl.ds(s * rows, rows), pl.ds(q * n_vir, n_vir))
            high_ref[at] = high
            low_ref[at] = low


def split_j(gathered, pair):
    shards, n_j, rows, n_vir = gathered.shape
    shape = (n_j // pair, shards * rows, pair * n_vir)
    block = pl.BlockSpec((1,) + shape[1:], lambda k: (k, 0, 0))
    return pl.pallas_call(
        split_j_kernel,
        grid=(n_j // pair,),
        in_specs=[pl.BlockSpec((shards, pair, rows, n_vir), lambda k: (0, k, 0, 0))],
        out_specs=[block, block],
        out_shape=[jax.ShapeDtypeStruct(shape, jnp.bfloat16)] * 2,
        compiler_params=pltpu.CompilerParams(vmem_limit_bytes=vmem_bytes),
        name="split_j",
    )(gathered)


def density_kernel(i_levels, j_levels, vir_ref, high_ref, low_ref, b_ref, out_ref,
                   at_high, at_low, amp_high, amp_low):
    shards, n_i, rows, n_vir = b_ref.shape
    n_aux = shards * rows
    pair = high_ref.shape[2] // n_vir
    step = pl.program_id(1)
    merge = 1
    while (merge * rows) % 128 and merge < shards:
        merge *= 2

    @pl.when(step == 0)
    def _():
        for i in range(n_i):
            for s in range(0, shards, merge):
                part = jnp.concatenate([b_ref[s + m, i] for m in range(merge)], 0)
                high, low = split_bf16(part.T)
                at = (pl.ds(i * n_vir, n_vir), pl.ds(s * rows, merge * rows))
                at_high[at] = high
                at_low[at] = low
        out_ref[...] = jnp.zeros_like(out_ref)

    for i in range(n_i):
        mine = pl.ds(i * n_vir, n_vir)
        ints = dot3(at_high[mine, :], at_low[mine, :], high_ref[0], low_ref[0])
        for q in range(pair):
            block = ints[:, q * n_vir:(q + 1) * n_vir]
            gaps = vir_ref[...] - (i_levels[pl.program_id(0) * n_i + i] + j_levels[step * pair + q])
            high, low = split_bf16((2.0 * block.T - block) / gaps)
            at = (pl.ds(q * n_vir, n_vir), mine)
            amp_high[at] = high
            amp_low[at] = low

    @pl.loop(0, shards // merge)
    def _(s):
        at = pl.ds(pl.multiple_of(s * (merge * rows), merge * rows), merge * rows)
        part = dot3(high_ref[0, at, :], low_ref[0, at, :], amp_high[...], amp_low[...])
        for m in range(merge):
            for i in range(n_i):
                out_ref[s * merge + m, i] += part[m * rows:(m + 1) * rows, i * n_vir:(i + 1) * n_vir]


def block_density(i_levels, j_levels, vir_pair, j_high, j_low, b_block):
    shards, n_i, rows, n_vir = b_block.shape
    steps, n_aux, width = j_high.shape
    at_once = 2 if n_i % 2 == 0 else 1
    smem = pl.BlockSpec(memory_space=pltpu.SMEM)
    vir_spec = pl.BlockSpec(vir_pair.shape, lambda h, k: (0, 0))
    j_spec = pl.BlockSpec((1, n_aux, width), lambda h, k: (k, 0, 0))
    b_spec = pl.BlockSpec((shards, at_once, rows, n_vir), lambda h, k: (0, h, 0, 0))
    flops = 2 * 2 * 3 * n_aux * n_i * n_vir * steps * width
    return pl.pallas_call(
        density_kernel,
        grid=(n_i // at_once, steps),
        in_specs=[smem, smem, vir_spec, j_spec, j_spec, b_spec],
        out_specs=b_spec,
        out_shape=jax.ShapeDtypeStruct(b_block.shape, jnp.float32),
        scratch_shapes=[
            pltpu.VMEM((at_once * n_vir, n_aux), jnp.bfloat16),
            pltpu.VMEM((at_once * n_vir, n_aux), jnp.bfloat16),
            pltpu.VMEM((width, at_once * n_vir), jnp.bfloat16),
            pltpu.VMEM((width, at_once * n_vir), jnp.bfloat16),
        ],
        compiler_params=pltpu.CompilerParams(vmem_limit_bytes=vmem_bytes),
        cost_estimate=pl.CostEstimate(
            flops=flops, bytes_accessed=4 * steps * n_aux * width + 8 * b_block.size,
            transcendentals=0),
        name="block_density",
    )(i_levels, j_levels, vir_pair, j_high, j_low, b_block)


def pack_kernel(_, __, in_ref, out_ref):
    out_ref[:, 0] = jnp.swapaxes(in_ref[...], 0, 1)


def block_of(m, which, owners):
    group, start, n_blocks = which[0], which[1], which[2]
    first = owners[jnp.maximum(group, 0)]
    return lax.rem(jnp.where(group < 0, 0, first) + start + m, n_blocks)


def pack(integrals, which, owners, n_i, width):
    rows, _, n_vir = integrals.shape
    cuts = 2 if rows % 16 == 0 else 1
    tile = rows // cuts
    return pl.pallas_call(
        pack_kernel,
        grid_spec=pltpu.PrefetchScalarGridSpec(
            num_scalar_prefetch=2,
            grid=(n_i, cuts),
            in_specs=[pl.BlockSpec((tile, width, n_vir), lambda m, r, *at: (r, block_of(m, *at), 0))],
            out_specs=pl.BlockSpec((width, 1, tile, n_vir), lambda m, r, *at: (0, m, r, 0)),
        ),
        out_shape=jax.ShapeDtypeStruct((width, n_i, rows, n_vir), jnp.float32),
        compiler_params=pltpu.CompilerParams(vmem_limit_bytes=vmem_bytes),
        cost_estimate=pl.CostEstimate(
            flops=0, bytes_accessed=8 * width * n_i * rows * n_vir, transcendentals=0),
        name="pack",
    )(which, owners, integrals)


def place_kernel(_, __, part_ref, *refs):
    out_ref = refs[-1]
    out_ref[...] = jnp.swapaxes(part_ref[:, 0], 0, 1)


def place(part, which, owners, out, shape):
    width, n_i, rows, n_vir = part.shape
    cuts = 2 if rows % 16 == 0 else 1
    tile = rows // cuts
    operands = [which, owners, part]
    in_specs = [pl.BlockSpec((width, 1, tile, n_vir), lambda m, r, *at: (0, m, r, 0))]
    aliases = {}
    if out is not None:
        operands.append(out)
        in_specs.append(pl.BlockSpec(memory_space=pl.ANY))
        aliases = {3: 0}
    return pl.pallas_call(
        place_kernel,
        grid_spec=pltpu.PrefetchScalarGridSpec(
            num_scalar_prefetch=2,
            grid=(n_i, cuts),
            in_specs=in_specs,
            out_specs=pl.BlockSpec((tile, width, n_vir), lambda m, r, *at: (r, block_of(m, *at), 0)),
        ),
        out_shape=jax.ShapeDtypeStruct(shape, jnp.float32),
        input_output_aliases=aliases,
        compiler_params=pltpu.CompilerParams(vmem_limit_bytes=vmem_bytes),
        cost_estimate=pl.CostEstimate(
            flops=0, bytes_accessed=8 * width * n_i * rows * n_vir, transcendentals=0),
        name="place",
    )(*operands)


def join_j_kernel(at_ref, *refs):
    high_ref, low_ref = refs[-2:]
    n_half = (len(refs) - 2) // 3
    near, cross, late = refs[:n_half], refs[n_half:2 * n_half], refs[2 * n_half:3 * n_half]
    rows, n_vir = near[0].shape[1:]
    step = pl.program_id(0)
    me = at_ref[0]
    far_start = (1 - me // n_half) * n_half

    def put(x, shard, q):
        high, low = split_bf16(x)
        at = (0, pl.ds(pl.multiple_of(shard * rows, rows), rows), pl.ds(q * n_vir, n_vir))
        high_ref[at] = high
        low_ref[at] = low

    for q in range(2):
        @pl.when(step % 2 == q)
        def _(q=q):
            for d in range(n_half):
                put(near[d][0], me ^ d, q)

            @pl.when(step < n_half)
            def _():
                for d in range(n_half):
                    put(cross[d][0], me ^ d ^ n_half, q)

            for d in range(n_half):
                if d % 2 == q:
                    @pl.when(step == n_half + d)
                    def _(d=d):
                        for s in range(n_half):
                            put(late[d][s], far_start + s, q)


def join_j(me, order, near, cross, late):
    n_half = len(near)
    n_j, rows, n_vir = near[0].shape
    shape = (n_j // 2, 2 * n_half * rows, 2 * n_vir)
    out_block = pl.BlockSpec((1,) + shape[1:], lambda k, at: (k // 2, 0, 0))
    in_specs = (
        [pl.BlockSpec((1, rows, n_vir), lambda k, at: (at[1 + k], 0, 0))] * n_half
        + [pl.BlockSpec((1, rows, n_vir), lambda k, at: (jnp.minimum(k, n_half - 1), 0, 0))] * n_half
        + [pl.BlockSpec((n_half, rows, n_vir), lambda k, at: (0, 0, 0))] * n_half
    )
    return pl.pallas_call(
        join_j_kernel,
        grid_spec=pltpu.PrefetchScalarGridSpec(
            num_scalar_prefetch=1,
            grid=(n_j,),
            in_specs=in_specs,
            out_specs=[out_block, out_block],
        ),
        out_shape=[jax.ShapeDtypeStruct(shape, jnp.bfloat16)] * 2,
        compiler_params=pltpu.CompilerParams(vmem_limit_bytes=vmem_bytes),
        cost_estimate=pl.CostEstimate(
            flops=0, bytes_accessed=8 * n_j * 2 * n_half * rows * n_vir, transcendentals=0),
        name="join_j",
    )(jnp.concatenate([me[None], order]), *near, *cross, *late)


def across(block, distance):
    route = [(i, i ^ distance) for i in range(lax.axis_size("aux"))]
    return lax.ppermute(block, "aux", route)


def within_half(block, n_half):
    found = [block]
    for d in range(1, n_half):
        low = d & -d
        found.append(across(found[d ^ low], low))
    return found


def pick(table, index):
    chosen = index[:, None] == jnp.arange(table.shape[0], dtype=jnp.int32)[None, :]
    return jnp.sum(jnp.where(chosen, table[None, :], 0.0), axis=1)


def body(integrals, occ_energy, vir_energy, orbital_order, owners):
    n_groups = lax.axis_size("grp")
    n_shards = lax.axis_size("aux")
    grp_index = lax.axis_index("grp").astype(jnp.int32)
    me = lax.axis_index("aux").astype(jnp.int32)
    rows, group_occ, n_vir = integrals.shape
    occ_block = group_occ // n_shards
    n_half = n_shards // 2
    shared = occ_block == n_shards and n_half >= 2 and n_shards & (n_shards - 1) == 0

    source_group = (grp_index + n_groups - 1) % n_groups
    next_group = (grp_index + 1) % n_groups
    my_owner = lax.dynamic_index_in_dim(owners[0], grp_index, 0, keepdims=False)
    next_owner = lax.dynamic_index_in_dim(owners[0], next_group, 0, keepdims=False)

    n_blocks = group_occ // n_shards
    first = next_owner if shared else jnp.int32(0)
    places = (first + jnp.arange(n_blocks, dtype=jnp.int32)) % n_blocks
    n_i = 2 if n_blocks % 2 == 0 else 1
    ends = [0, n_i, n_blocks - n_i, n_blocks] if n_blocks >= 3 * n_i else [0, n_blocks]
    planned = next_group if shared else jnp.int32(-1)
    chunks = [(jnp.stack([planned, jnp.int32(start), jnp.int32(n_blocks)]), owners[0], end - start)
              for start, end in zip(ends, ends[1:])]

    def send_in(part):
        return lax.all_to_all(part, "aux", split_axis=0, concat_axis=0, tiled=True)

    parts = [pack(integrals, *chunk, n_shards) for chunk in chunks]
    blocks = [send_in(parts[0])]
    sent = lax.dynamic_slice_in_dim(integrals, next_owner * occ_block, occ_block, 1)
    arrived = from_behind(jnp.transpose(sent, (1, 0, 2)), "grp", 1)
    if len(parts) > 1:
        bound = lax.optimization_barrier((arrived, *parts[1:]))
        arrived, parts[1:] = bound[0], bound[1:]

    def send_after(c, *done):
        if c < len(parts):
            part = lax.optimization_barrier((parts[c], blocks[c - 1]) + done)[0]
            blocks.append(send_in(part))

    natural = jnp.arange(occ_block, dtype=jnp.int32)
    if shared:
        half = me // n_half
        far_start = (1 - half) * n_half
        near = within_half(arrived, n_half)
        crossing = lax.dynamic_slice_in_dim(arrived, half * n_half, n_half, 0)
        crossed = across(crossing, n_half)
        send_after(1, near[n_half // 2], crossed)
        owned = lax.dynamic_slice(
            blocks[0], (far_start, 0, 0, 0), (n_half, 1, rows, n_vir)).reshape(n_half, rows, n_vir)
        late_own = from_behind(owned, "grp", 1)
        crossed = lax.optimization_barrier((crossed, late_own))[0]
        cross = within_half(crossed, n_half)
        late = within_half(late_own, n_half)
        send_after(2, late[n_half // 2], cross[n_half // 2])
        order = jnp.where(natural < n_half, far_start + natural, me ^ (natural - n_half))
        j_high, j_low = join_j(me, order, near, cross, late)
    else:
        order = natural
        gathered = lax.all_gather(arrived, "aux", axis=0, tiled=False)
        j_high, j_low = split_j(gathered, 2 if occ_block % 2 == 0 else 1)
    for c in range(len(blocks), len(parts)):
        send_after(c)

    levels = pick(occ_energy, orbital_order)
    vir_pair = vir_energy[:, None] + vir_energy[None, :] + level_shift
    j_levels = pick(levels, source_group * group_occ + my_owner * occ_block + order)
    i_levels = pick(levels, grp_index * group_occ + places * n_shards + me)

    out = None
    for c, (chunk, block) in enumerate(zip(chunks, blocks)):
        density = block_density(
            i_levels[ends[c]:ends[c + 1]], j_levels, vir_pair, j_high, j_low, block)
        density = lax.optimization_barrier((density, blocks[-1]))[0]
        back = lax.all_to_all(density, "aux", split_axis=0, concat_axis=0, tiled=True)
        out = place(back, *chunk[:2], out, integrals.shape)
    return out


def solution(mesh):
    in_specs = (P("aux", "grp", None), P(), P(), P(), P())
    out_specs = P("aux", "grp", None)
    return jax.shard_map(body, mesh=mesh, in_specs=in_specs, out_specs=out_specs, check_vma=False)
```

```python
import jax
import jax.numpy as jnp
from jax import lax
from jax.experimental import pallas as pl
from jax.experimental.pallas import tpu as pltpu
from jax.sharding import PartitionSpec as P

level_shift = 0.5
vmem_bytes = 56 * 1024 * 1024


def from_behind(block, axis, distance):
    devices = range(lax.axis_size(axis))
    route = [((i - distance) % len(devices), i) for i in devices]
    return lax.ppermute(block, axis, route)


def split_bf16(x):
    high = x.astype(jnp.bfloat16)
    low = (x - high.astype(jnp.float32)).astype(jnp.bfloat16)
    return high, low


def dot3(a_high, a_low, b_high, b_low):
    def dot(a, b):
        return jnp.dot(a, b, preferred_element_type=jnp.float32)

    return dot(a_high, b_high) + (dot(a_high, b_low) + dot(a_low, b_high))


def split_j_kernel(j_ref, high_ref, low_ref):
    shards, pair, rows, n_vir = j_ref.shape
    for s in range(shards):
        for q in range(pair):
            high, low = split_bf16(j_ref[s, q])
            at = (0, pl.ds(s * rows, rows), pl.ds(q * n_vir, n_vir))
            high_ref[at] = high
            low_ref[at] = low


def split_j(gathered, pair):
    shards, n_j, rows, n_vir = gathered.shape
    shape = (n_j // pair, shards * rows, pair * n_vir)
    block = pl.BlockSpec((1,) + shape[1:], lambda k: (k, 0, 0))
    return pl.pallas_call(
        split_j_kernel,
        grid=(n_j // pair,),
        in_specs=[pl.BlockSpec((shards, pair, rows, n_vir), lambda k: (0, k, 0, 0))],
        out_specs=[block, block],
        out_shape=[jax.ShapeDtypeStruct(shape, jnp.bfloat16)] * 2,
        compiler_params=pltpu.CompilerParams(vmem_limit_bytes=vmem_bytes),
        name="split_j",
    )(gathered)


def density_kernel(i_levels, j_levels, vir_ref, high_ref, low_ref, b_ref, out_ref,
                   at_high, at_low, amp_high, amp_low):
    shards, n_i, rows, n_vir = b_ref.shape
    n_aux = shards * rows
    pair = high_ref.shape[2] // n_vir
    step = pl.program_id(1)
    merge = 1
    while (merge * rows) % 128 and merge < shards:
        merge *= 2

    @pl.when(step == 0)
    def _():
        for i in range(n_i):
            for s in range(0, shards, merge):
                part = jnp.concatenate([b_ref[s + m, i] for m in range(merge)], 0)
                high, low = split_bf16(part.T)
                at = (pl.ds(i * n_vir, n_vir), pl.ds(s * rows, merge * rows))
                at_high[at] = high
                at_low[at] = low
        out_ref[...] = jnp.zeros_like(out_ref)

    for i in range(n_i):
        mine = pl.ds(i * n_vir, n_vir)
        ints = dot3(at_high[mine, :], at_low[mine, :], high_ref[0], low_ref[0])
        for q in range(pair):
            block = ints[:, q * n_vir:(q + 1) * n_vir]
            gaps = vir_ref[...] - (i_levels[pl.program_id(0) * n_i + i] + j_levels[step * pair + q])
            high, low = split_bf16((2.0 * block.T - block) / gaps)
            at = (pl.ds(q * n_vir, n_vir), mine)
            amp_high[at] = high
            amp_low[at] = low

    group = merge * (2 if (shards // merge) % 2 == 0 else 1)

    @pl.loop(0, shards // group)
    def _(s):
        at = pl.ds(pl.multiple_of(s * (group * rows), group * rows), group * rows)
        part = dot3(high_ref[0, at, :], low_ref[0, at, :], amp_high[...], amp_low[...])
        for m in range(group):
            for i in range(n_i):
                out_ref[s * group + m, i] += part[m * rows:(m + 1) * rows, i * n_vir:(i + 1) * n_vir]


def block_density(i_levels, j_levels, vir_pair, j_high, j_low, b_block):
    shards, n_i, rows, n_vir = b_block.shape
    steps, n_aux, width = j_high.shape
    at_once = 2 if n_i % 2 == 0 else 1
    smem = pl.BlockSpec(memory_space=pltpu.SMEM)
    vir_spec = pl.BlockSpec(vir_pair.shape, lambda h, k: (0, 0))
    j_spec = pl.BlockSpec((1, n_aux, width), lambda h, k: (k, 0, 0))
    b_spec = pl.BlockSpec((shards, at_once, rows, n_vir), lambda h, k: (0, h, 0, 0))
    flops = 2 * 2 * 3 * n_aux * n_i * n_vir * steps * width
    return pl.pallas_call(
        density_kernel,
        grid=(n_i // at_once, steps),
        in_specs=[smem, smem, vir_spec, j_spec, j_spec, b_spec],
        out_specs=b_spec,
        out_shape=jax.ShapeDtypeStruct(b_block.shape, jnp.float32),
        scratch_shapes=[
            pltpu.VMEM((at_once * n_vir, n_aux), jnp.bfloat16),
            pltpu.VMEM((at_once * n_vir, n_aux), jnp.bfloat16),
            pltpu.VMEM((width, at_once * n_vir), jnp.bfloat16),
            pltpu.VMEM((width, at_once * n_vir), jnp.bfloat16),
        ],
        compiler_params=pltpu.CompilerParams(vmem_limit_bytes=vmem_bytes),
        cost_estimate=pl.CostEstimate(
            flops=flops, bytes_accessed=4 * steps * n_aux * width + 8 * b_block.size,
            transcendentals=0),
        name="block_density",
    )(i_levels, j_levels, vir_pair, j_high, j_low, b_block)


def pack_kernel(_, __, in_ref, out_ref):
    out_ref[:, 0] = jnp.swapaxes(in_ref[...], 0, 1)


def block_of(m, which, owners):
    group, start, n_blocks = which[0], which[1], which[2]
    first = owners[jnp.maximum(group, 0)]
    return lax.rem(jnp.where(group < 0, 0, first) + start + m, n_blocks)


def pack(integrals, which, owners, n_i, width):
    rows, _, n_vir = integrals.shape
    cuts = 2 if rows % 16 == 0 else 1
    tile = rows // cuts
    return pl.pallas_call(
        pack_kernel,
        grid_spec=pltpu.PrefetchScalarGridSpec(
            num_scalar_prefetch=2,
            grid=(n_i, cuts),
            in_specs=[pl.BlockSpec((tile, width, n_vir), lambda m, r, *at: (r, block_of(m, *at), 0))],
            out_specs=pl.BlockSpec((width, 1, tile, n_vir), lambda m, r, *at: (0, m, r, 0)),
        ),
        out_shape=jax.ShapeDtypeStruct((width, n_i, rows, n_vir), jnp.float32),
        compiler_params=pltpu.CompilerParams(vmem_limit_bytes=vmem_bytes),
        cost_estimate=pl.CostEstimate(
            flops=0, bytes_accessed=8 * width * n_i * rows * n_vir, transcendentals=0),
        name="pack",
    )(which, owners, integrals)


def place_kernel(_, __, part_ref, *refs):
    out_ref = refs[-1]
    out_ref[...] = jnp.swapaxes(part_ref[:, 0], 0, 1)


def place(part, which, owners, out, shape):
    width, n_i, rows, n_vir = part.shape
    cuts = 2 if rows % 16 == 0 else 1
    tile = rows // cuts
    operands = [which, owners, part]
    in_specs = [pl.BlockSpec((width, 1, tile, n_vir), lambda m, r, *at: (0, m, r, 0))]
    aliases = {}
    if out is not None:
        operands.append(out)
        in_specs.append(pl.BlockSpec(memory_space=pl.ANY))
        aliases = {3: 0}
    return pl.pallas_call(
        place_kernel,
        grid_spec=pltpu.PrefetchScalarGridSpec(
            num_scalar_prefetch=2,
            grid=(n_i, cuts),
            in_specs=in_specs,
            out_specs=pl.BlockSpec((tile, width, n_vir), lambda m, r, *at: (r, block_of(m, *at), 0)),
        ),
        out_shape=jax.ShapeDtypeStruct(shape, jnp.float32),
        input_output_aliases=aliases,
        compiler_params=pltpu.CompilerParams(vmem_limit_bytes=vmem_bytes),
        cost_estimate=pl.CostEstimate(
            flops=0, bytes_accessed=8 * width * n_i * rows * n_vir, transcendentals=0),
        name="place",
    )(*operands)


def join_j_kernel(at_ref, *refs):
    high_ref, low_ref = refs[-2:]
    n_half = (len(refs) - 2) // 3
    near, cross, late = refs[:n_half], refs[n_half:2 * n_half], refs[2 * n_half:3 * n_half]
    rows, n_vir = near[0].shape[1:]
    step = pl.program_id(0)
    me = at_ref[0]
    far_start = (1 - me // n_half) * n_half

    def put(x, shard, q):
        high, low = split_bf16(x)
        at = (0, pl.ds(pl.multiple_of(shard * rows, rows), rows), pl.ds(q * n_vir, n_vir))
        high_ref[at] = high
        low_ref[at] = low

    for q in range(2):
        @pl.when(step % 2 == q)
        def _(q=q):
            for d in range(n_half):
                put(near[d][0], me ^ d, q)

            @pl.when(step < n_half)
            def _():
                for d in range(n_half):
                    put(cross[d][0], me ^ d ^ n_half, q)

            for d in range(n_half):
                if d % 2 == q:
                    @pl.when(step == n_half + d)
                    def _(d=d):
                        for s in range(n_half):
                            put(late[d][s], far_start + s, q)


def join_j(me, order, near, cross, late):
    n_half = len(near)
    n_j, rows, n_vir = near[0].shape
    shape = (n_j // 2, 2 * n_half * rows, 2 * n_vir)
    out_block = pl.BlockSpec((1,) + shape[1:], lambda k, at: (k // 2, 0, 0))
    in_specs = (
        [pl.BlockSpec((1, rows, n_vir), lambda k, at: (at[1 + k], 0, 0))] * n_half
        + [pl.BlockSpec((1, rows, n_vir), lambda k, at: (jnp.minimum(k, n_half - 1), 0, 0))] * n_half
        + [pl.BlockSpec((n_half, rows, n_vir), lambda k, at: (0, 0, 0))] * n_half
    )
    return pl.pallas_call(
        join_j_kernel,
        grid_spec=pltpu.PrefetchScalarGridSpec(
            num_scalar_prefetch=1,
            grid=(n_j,),
            in_specs=in_specs,
            out_specs=[out_block, out_block],
        ),
        out_shape=[jax.ShapeDtypeStruct(shape, jnp.bfloat16)] * 2,
        compiler_params=pltpu.CompilerParams(vmem_limit_bytes=vmem_bytes),
        cost_estimate=pl.CostEstimate(
            flops=0, bytes_accessed=8 * n_j * 2 * n_half * rows * n_vir, transcendentals=0),
        name="join_j",
    )(jnp.concatenate([me[None], order]), *near, *cross, *late)


def across(block, distance):
    route = [(i, i ^ distance) for i in range(lax.axis_size("aux"))]
    return lax.ppermute(block, "aux", route)


def within_half(block, n_half):
    found = [block]
    for d in range(1, n_half):
        low = d & -d
        found.append(across(found[d ^ low], low))
    return found


def pick(table, index):
    chosen = index[:, None] == jnp.arange(table.shape[0], dtype=jnp.int32)[None, :]
    return jnp.sum(jnp.where(chosen, table[None, :], 0.0), axis=1)


def body(integrals, occ_energy, vir_energy, orbital_order, owners):
    n_groups = lax.axis_size("grp")
    n_shards = lax.axis_size("aux")
    grp_index = lax.axis_index("grp").astype(jnp.int32)
    me = lax.axis_index("aux").astype(jnp.int32)
    rows, group_occ, n_vir = integrals.shape
    occ_block = group_occ // n_shards
    n_half = n_shards // 2
    shared = occ_block == n_shards and n_half >= 2 and n_shards & (n_shards - 1) == 0

    source_group = (grp_index + n_groups - 1) % n_groups
    next_group = (grp_index + 1) % n_groups
    my_owner = lax.dynamic_index_in_dim(owners[0], grp_index, 0, keepdims=False)
    next_owner = lax.dynamic_index_in_dim(owners[0], next_group, 0, keepdims=False)

    n_blocks = group_occ // n_shards
    first = next_owner if shared else jnp.int32(0)
    places = (first + jnp.arange(n_blocks, dtype=jnp.int32)) % n_blocks
    n_i = 2 if n_blocks % 2 == 0 else 1
    ends = [0, n_i, n_blocks - n_i, n_blocks] if n_blocks >= 3 * n_i else [0, n_blocks]
    planned = next_group if shared else jnp.int32(-1)
    chunks = [(jnp.stack([planned, jnp.int32(start), jnp.int32(n_blocks)]), owners[0], end - start)
              for start, end in zip(ends, ends[1:])]

    def send_in(part):
        return lax.all_to_all(part, "aux", split_axis=0, concat_axis=0, tiled=True)

    parts = [pack(integrals, *chunk, n_shards) for chunk in chunks]
    blocks = [send_in(parts[0])]
    sent = lax.dynamic_slice_in_dim(integrals, next_owner * occ_block, occ_block, 1)
    arrived = from_behind(jnp.transpose(sent, (1, 0, 2)), "grp", 1)
    if len(parts) > 1:
        bound = lax.optimization_barrier((arrived, *parts[1:]))
        arrived, parts[1:] = bound[0], bound[1:]

    def send_after(c, *done):
        if c < len(parts):
            part = lax.optimization_barrier((parts[c], blocks[c - 1]) + done)[0]
            blocks.append(send_in(part))

    natural = jnp.arange(occ_block, dtype=jnp.int32)
    if shared:
        half = me // n_half
        far_start = (1 - half) * n_half
        near = within_half(arrived, n_half)
        crossing = lax.dynamic_slice_in_dim(arrived, half * n_half, n_half, 0)
        crossed = across(crossing, n_half)
        send_after(1, near[n_half // 2], crossed)
        owned = lax.dynamic_slice(
            blocks[0], (far_start, 0, 0, 0), (n_half, 1, rows, n_vir)).reshape(n_half, rows, n_vir)
        late_own = from_behind(owned, "grp", 1)
        crossed = lax.optimization_barrier((crossed, late_own))[0]
        cross = within_half(crossed, n_half)
        late = within_half(late_own, n_half)
        send_after(2, late[n_half // 2], cross[n_half // 2])
        order = jnp.where(natural < n_half, far_start + natural, me ^ (natural - n_half))
        j_high, j_low = join_j(me, order, near, cross, late)
    else:
        order = natural
        gathered = lax.all_gather(arrived, "aux", axis=0, tiled=False)
        j_high, j_low = split_j(gathered, 2 if occ_block % 2 == 0 else 1)
    for c in range(len(blocks), len(parts)):
        send_after(c)

    levels = pick(occ_energy, orbital_order)
    vir_pair = vir_energy[:, None] + vir_energy[None, :] + level_shift
    j_levels = pick(levels, source_group * group_occ + my_owner * occ_block + order)
    i_levels = pick(levels, grp_index * group_occ + places * n_shards + me)

    out = None
    for c, (chunk, block) in enumerate(zip(chunks, blocks)):
        density = block_density(
            i_levels[ends[c]:ends[c + 1]], j_levels, vir_pair, j_high, j_low, block)
        density = lax.optimization_barrier((density, blocks[-1]))[0]
        back = lax.all_to_all(density, "aux", split_axis=0, concat_axis=0, tiled=True)
        out = place(back, *chunk[:2], out, integrals.shape)
    return out


def solution(mesh):
    in_specs = (P("aux", "grp", None), P(), P(), P(), P())
    out_specs = P("aux", "grp", None)
    return jax.shard_map(body, mesh=mesh, in_specs=in_specs, out_specs=out_specs, check_vma=False)
```
